128 devices in a mesh: row: 8 (over x, core), col: 16 (over z, y).
Axes of the slice: x: 4, y: 4, z: 4, core: 2. Of those that a mesh axis runs over, the one named last changes fastest.
Arguments:
- child_update: bfloat16 [16, 8, 128, 8, 16, 128], P(None, 'row', None, None, 'col'), may hold values from -6 to 6
- child_panel: bfloat16 [16, 8, 128, 512], P(None, 'row', None, 'col'), may hold values from -1.1953125 to 1.1953125
- front: bfloat16 [24, 8, 128, 12, 16, 128], P(None, 'row', None, None, 'col'), may hold values from -6 to 6
- diag_inverse: bfloat16 [512, 512], replicated, may hold values from -0.0625 to 0.0625
- parent_tile: int32 [128], replicated, may hold values from 0 to 191, as said below
Outputs:
- panel: bfloat16 [24, 8, 128, 16, 32], P(None, 'row', None, 'col')
- updated_front: bfloat16 [24, 8, 128, 12, 16, 128], P(None, 'row', None, None, 'col')
The draws below stay inside these ranges and needn't reach their ends.
Inputs may be any that keep to these rules, and one draw needn't show every extreme that they name: `parent_tile`: all values are distinct. Tile t lives on process row t mod 8 and process column t mod 16. The child tiles of one process row (equal a mod 8) send exactly 2 to each process row; the child tiles of one process column (equal a mod 16) send at most 1 to any process column, and exactly 1 to some.
All inputs are finite; a program needn't handle non-finite values.
Results may differ from the reference program's by a relative error of at most 0.0068.
Values may be sent and summed in bfloat16 or wider, within the bound.
A program may use at most 256 MiB of HBM per device.

```python
import jax
import jax.numpy as jnp
from jax import lax

NC = 16384
NP = 24576
W = 512
TILE = 128
NCT = 128
CR = 16
CCOL = 8
PR = 24
PC = 12
N_ROW = 8
N_COL = 16


def ensure_first(shuffled, target):
    position = jnp.argmax(shuffled == target)
    leading = shuffled[0]
    swapped = jnp.where(jnp.arange(shuffled.shape[0]) == position, leading, shuffled)
    return swapped.at[0].set(target)


def draw_parent_tile(key, part):
    per_column = NCT // N_COL
    fold_count = N_COL // N_ROW
    slot_count = NP // (TILE * N_COL)
    key_order, key_lift, key_slots = jax.random.split(key, 3)
    shuffled = jax.random.permutation(key_order, per_column)
    lifted = jax.random.randint(key_lift, (N_ROW,), 0, fold_count)
    residue = shuffled % N_ROW
    upper = (shuffled // N_ROW + lifted[residue]) % fold_count
    offsets = residue + N_ROW * upper
    child_ids = jnp.arange(NCT)
    owner_col = (child_ids % N_COL + offsets[child_ids // N_COL]) % N_COL

    def shuffle_slots(subkey):
        return jax.random.permutation(subkey, slot_count)
    tables = jax.vmap(shuffle_slots)(jax.random.split(key_slots, N_COL))
    tables = tables.at[0].set(ensure_first(tables[0], 0))
    tables = tables.at[N_COL - 1].set(ensure_first(tables[N_COL - 1], slot_count - 1))
    chosen = tables[owner_col, child_ids // N_COL]
    return (owner_col + N_COL * chosen).astype(jnp.int32)


def levels(own_key, shape, pieces, smallest, top_value):
    def one(axis_at, shards_of):
        heights = jax.random.uniform(jax.random.fold_in(jax.random.fold_in(own_key, 6), axis_at), (shards_of,), jnp.float32, smallest / len(pieces), top_value / len(pieces))
        return jnp.repeat(jnp.exp(heights), shape[axis_at] // shards_of).reshape((-1,) + (1,) * (len(shape) - axis_at - 1))

    level = one(*pieces[0])
    for cut in pieces[1:]:
        level = level * one(*cut)
    return level


def gaussian(key, extent, scale, most, shards=(), kind=jnp.bfloat16):
    drawn = jax.random.normal(key, extent, jnp.float32) * scale
    if len(shards) > 0:
        drawn = levels(key, extent, shards, -0.22, 0.18) * drawn
    return jnp.clip(drawn, min=-most, max=most).astype(kind)


def setup_inputs(seed: int = 0) -> dict:
    arg_keys = jax.random.split(jax.random.key(seed), 6)
    child_update = gaussian(arg_keys[0], (CR, N_ROW, TILE, CCOL, N_COL, TILE), 1.0, 6.0, ((1, 8), (4, 16)))
    child_panel = gaussian(arg_keys[1], (CR, N_ROW, TILE, W), 0.2, 1.1953125, ((1, 8), (3, 16)))
    front = gaussian(arg_keys[2], (PR, N_ROW, TILE, PC, N_COL, TILE), 1.0, 6.0, ((1, 8), (4, 16)))
    diag_inverse = gaussian(arg_keys[3], (W, W), (16 * W) ** -0.5, 0.0625)
    parent_tile = draw_parent_tile(jax.random.fold_in(arg_keys[5], 71), 0)
    return {"child_update": child_update, "child_panel": child_panel, "front": front, "diag_inverse": diag_inverse, "parent_tile": parent_tile}


def reference(child_update, child_panel, front, diag_inverse, parent_tile):
    child_rows = child_panel.reshape(NC, W)
    update_matrix = child_update.reshape(NC, NC)
    assembled = front.reshape(NP, NP)
    offsets = jnp.arange(TILE, dtype=jnp.int32)
    column_index = (parent_tile[:, None] * TILE + offsets[None, :]).reshape(NC).astype(jnp.int32)

    def add_tile(child_tile, current):
        first_row = (jnp.asarray(child_tile, jnp.int32) * TILE).astype(jnp.int32)
        update_rows = lax.dynamic_slice_in_dim(update_matrix, first_row, TILE, 0)
        panel_rows = lax.dynamic_slice_in_dim(child_rows, first_row, TILE, 0)
        schur_rows = (update_rows.astype(jnp.float32) - jnp.dot(panel_rows, child_rows.T, preferred_element_type=jnp.float32)).astype(jnp.bfloat16)
        target_row = (parent_tile[child_tile] * TILE).astype(jnp.int32)
        block = lax.dynamic_slice_in_dim(current, target_row, TILE, 0)
        block = block.astype(jnp.float32).at[:, column_index].add(schur_rows.astype(jnp.float32)).astype(jnp.bfloat16)
        return lax.dynamic_update_slice_in_dim(current, block, target_row, 0)

    assembled = lax.fori_loop(0, NC // TILE, add_tile, assembled)
    panel = jnp.dot(assembled[:, :W], diag_inverse, preferred_element_type=jnp.float32).astype(jnp.bfloat16)
    global_cols = jnp.arange(NP, dtype=jnp.int32)

    def renew_rows(parent_row):
        first_row = (parent_row * TILE).astype(jnp.int32)
        current_rows = lax.dynamic_slice_in_dim(assembled, first_row, TILE, 0)
        panel_rows = lax.dynamic_slice_in_dim(panel, first_row, TILE, 0)
        product = jnp.dot(panel_rows, panel.T, preferred_element_type=jnp.float32)
        renewed = (current_rows.astype(jnp.float32) - product).astype(jnp.bfloat16)
        trailing = (first_row >= W) & (global_cols[None, :] >= W)
        return jnp.where(trailing, renewed, current_rows)

    blocks = lax.map(renew_rows, jnp.arange(NP // TILE, dtype=jnp.int32))
    updated_front = blocks.reshape(NP, NP).reshape(PR, N_ROW, TILE, PC, N_COL, TILE)
    return panel.reshape(PR, N_ROW, TILE, N_COL, W // N_COL), updated_front
```

```python
import jax
import jax.numpy as jnp
from jax import lax
from jax.experimental import pallas as pl
from jax.experimental.pallas import tpu as pltpu
from jax.sharding import PartitionSpec as P

MESH = pl.DeviceIdType.MESH
BF = jnp.bfloat16
F32 = jnp.float32
ROWS = [(1, 0), (3, 0), (1, 1), (3, 1), (2, 0), (2, 1), (0, 1)]
RING = [1, 3, 2]
N_SEMS = 240


def tables(parent_tile, row, col):
    ids = jnp.arange(128, dtype=jnp.int32)
    mine_rows = lax.dynamic_index_in_dim(parent_tile.reshape(16, 8), row, 1, keepdims=False) % 8
    slots = jnp.arange(16, dtype=jnp.int32)
    to_row = mine_rows[None, :] == jnp.arange(8, dtype=jnp.int32)[:, None]
    first = jnp.min(jnp.where(to_row, slots[None, :], 15), axis=1)
    last = jnp.max(jnp.where(to_row, slots[None, :], 0), axis=1)
    row_order = jnp.stack([first, last], axis=1).reshape(16)
    mine_cols = lax.dynamic_index_in_dim(parent_tile.reshape(8, 16), col, 1, keepdims=False) % 16
    to_col = mine_cols[None, :] == slots[:, None]
    col_order = jnp.sum(jnp.where(to_col, jnp.arange(8, dtype=jnp.int32)[None, :], 0), axis=1)
    here = parent_tile % 8 == row
    lowest = jnp.min(jnp.where(here, ids, 999).reshape(16, 8), axis=0)
    rank = (ids.reshape(16, 8) != lowest[None, :]).reshape(128).astype(jnp.int32)
    row_match = parent_tile[None, :] == (row + 8 * jnp.arange(24, dtype=jnp.int32))[:, None]
    row_from = jnp.sum(jnp.where(row_match, (rank * 8 + ids % 8)[None, :], 0), axis=1)
    row_ok = jnp.any(row_match, axis=1).astype(jnp.int32)
    col_match = parent_tile[None, :] == (col + 16 * jnp.arange(12, dtype=jnp.int32))[:, None]
    col_from = jnp.sum(jnp.where(col_match, (ids % 16)[None, :], 0), axis=1)
    col_ok = jnp.any(col_match, axis=1).astype(jnp.int32)
    return jnp.concatenate([row_order, col_order, row_from, row_ok, col_from, col_ok]).astype(jnp.int32)


T_COL, T_RFROM, T_ROK, T_CFROM, T_COK = 16, 32, 56, 80, 92


def arrived_tile(tab, arr, i, j):
    source_row = tab[T_RFROM + i]
    rank, q = source_row // 8, source_row % 8
    half, place = q // 4, q % 4
    source = tab[T_CFROM + j]
    lo, hi = source // 4, source % 4
    major = jnp.where(half == 0, hi, lo)
    minor = jnp.where(half == 0, lo, hi)
    upper = arr[rank * 2, half, major, minor, place]
    lower = arr[rank * 2 + 1, half, major, minor, place]
    ok = (tab[T_ROK + i] * tab[T_COK + j]) == 1
    tile = jnp.concatenate([upper, lower], axis=0).astype(F32)
    return jnp.where(ok, tile, jnp.zeros_like(tile))


def exchange(
    tab, u, gt, front, dinv, arr_out, prow, pcol,
    us, ux, g1s, g1r, rowg, rowt, cmid, colt, colgr, colga, colgb, uf, sc, s1, mid, arr, fp, extc, eq, ep,
    lsem, ssem, rsem,
):
    r, c = lax.axis_index("row"), lax.axis_index("col")
    x, k, z, y = r // 2, r % 2, c // 4, c % 4
    counter = [0]
    pending = []

    def row_dev(dx, dk):
        return ((x + dx) % 4) * 2 + (k + dk) % 2

    def row_from(dx, dk):
        return ((x + 4 - dx) % 4) * 2 + (k + dk) % 2

    def sem():
        counter[0] += 1
        return counter[0] - 1

    def send(src, dst, dev, landing):
        n = sem()
        out = pltpu.make_async_remote_copy(src, dst, ssem.at[n], rsem.at[n], device_id=dev, device_id_type=MESH)
        out.start()
        pending.append(out)
        return pltpu.make_async_remote_copy(landing, landing, ssem.at[n], rsem.at[n], device_id=dev, device_id_type=MESH)

    def arrive(waits):
        for w in waits:
            w.wait_recv()

    def local(src, dst):
        n = sem()
        copy = pltpu.make_async_copy(src, dst, lsem.at[n])
        copy.start()
        return copy

    def to_z(d):
        return (r, ((z + d) % 4) * 4 + y)

    def to_y(d):
        return (r, z * 4 + (y + d) % 4)

    for rp in range(8):
        g1s[rp, 0] = gt[tab[2 * rp]]
        g1s[rp, 1] = gt[tab[2 * rp + 1]]
        g1s[rp, 2] = gt[2 * rp]
        g1s[rp, 3] = gt[2 * rp + 1]

    barrier = pltpu.get_barrier_semaphore()
    for dx, dk in ROWS:
        pl.semaphore_signal(barrier, inc=1, device_id=(row_dev(dx, dk), c), device_id_type=MESH)
    for d in RING:
        pl.semaphore_signal(barrier, inc=1, device_id=to_z(d), device_id_type=MESH)
        pl.semaphore_signal(barrier, inc=1, device_id=to_y(d), device_id_type=MESH)
    pl.semaphore_wait(barrier, 13)

    g1 = [
        send(g1s.at[row_dev(dx, dk)], g1r.at[r], (row_dev(dx, dk), c), g1r.at[row_from(dx, dk)])
        for dx, dk in ROWS
    ]
    g1r[r] = g1s[r]

    @pl.loop(0, 16)
    def _(n):
        us[n // 2, n % 2] = u[tab[n]]

    ux[r] = us[r]

    def send_child(part):
        rank, rows = part // 2, pl.ds((part % 2) * 512, 512)
        return [
            send(
                us.at[row_dev(dx, dk), rank, rows], ux.at[r, rank, rows], (row_dev(dx, dk), c),
                ux.at[row_from(dx, dk), rank, rows],
            )
            for dx, dk in ROWS
        ]

    child = {0: send_child(0)}
    copies = []

    arrive(g1)
    yz, zy = pl.ds((y * 4 + z) * 32, 32), pl.ds((z * 4 + y) * 32, 32)

    def col_piece(zp):
        return g1r.at[pl.ds(4 * (zp % 2), 4), 2 + zp // 2]

    c1 = [send(col_piece((z + d) % 4), cmid.at[z], to_z(d), cmid.at[(z + 4 - d) % 4]) for d in RING]
    own = [
        local(col_piece(z), cmid.at[z]),
        local(g1r.at[:, 0], rowg.at[0, :, yz]),
        local(g1r.at[:, 1], rowg.at[1, :, zy]),
    ]
    a1 = [
        send(g1r.at[:, 0], rowg.at[0, :, yz], to_z(d), rowg.at[0, :, pl.ds((y * 4 + (z + 4 - d) % 4) * 32, 32)])
        for d in RING
    ]
    b1 = [
        send(g1r.at[:, 1], rowg.at[1, :, zy], to_y(d), rowg.at[1, :, pl.ds((z * 4 + (y + 4 - d) % 4) * 32, 32)])
        for d in RING
    ]
    for copy in own:
        copy.wait()
    arrive(c1)
    c2 = [send(cmid.at[:, (y + d) % 4], colt.at[y], to_y(d), colt.at[(y + 4 - d) % 4]) for d in RING]
    mine = local(cmid.at[:, y], colt.at[y])
    arrive(a1)
    y128, z128 = pl.ds(y * 128, 128), pl.ds(z * 128, 128)
    a2 = [
        send(rowg.at[0, :, y128], rowg.at[0, :, y128], to_y(d), rowg.at[0, :, pl.ds((y + 4 - d) % 4 * 128, 128)])
        for d in RING
    ]
    arrive(b1)
    b2 = [
        send(rowg.at[1, :, z128], rowg.at[1, :, z128], to_z(d), rowg.at[1, :, pl.ds((z + 4 - d) % 4 * 128, 128)])
        for d in RING
    ]
    mine.wait()
    arrive(c2)
    d1 = [send(colt, colgr.at[r], (row_dev(d, 0), c), colgr.at[row_from(d, 0)]) for d in RING]
    local(colt, colgr.at[r]).wait()
    arrive(d1)
    sibling = (row_dev(0, 1), c)
    d2 = [send(colgr.at[2 * q + k], colgr.at[2 * q + k], sibling, colgr.at[2 * q + 1 - k]) for q in range(4)]
    child[1] = send_child(1)
    arrive(d2)
    for j in range(8):
        for a in range(4):
            for b in range(4):
                piece = colgr[j, a, b]
                colga[pl.ds((a * 4 + b) * 32, 32), pl.ds(j * 128, 128)] = piece
                colgb[pl.ds((b * 4 + a) * 32, 32), pl.ds(j * 128, 128)] = piece

    def turn(rank):
        @pl.loop(0, 8)
        def _(q):
            turned = rowg[rank, q].T
            rowt[2 * rank, q] = turned[0:64]
            rowt[2 * rank + 1, q] = turned[64:128]

    def schur(part, half):
        rank = part // 2
        colg = colga if rank == 0 else colgb

        @pl.loop(0, 4)
        def _(q):
            uf[pl.ds(q * 512, 512)] = ux[half * 4 + q, rank, pl.ds((part % 2) * 512, 512)].astype(F32)

        left = rowt.at[part, pl.ds(half * 4, 4)]

        for n in range(4):
            prod = jnp.dot(
                left[...].reshape(256, 512), colg[:, n * 256 : n * 256 + 256], preferred_element_type=F32
            )
            for e in range(2):
                j = 2 * n + e
                sc[j] = (uf[pl.ds(j, 256, stride=8), :] - prod[:, e * 128 : e * 128 + 128]).astype(BF)

        @pl.loop(0, 16)
        def _(t):
            lo, hi = t // 4, t % 4
            if half == 0:
                s1[part, half, lo, hi] = sc[tab[T_COL + t]].reshape(4, 64, 128)
            else:
                s1[part, half, hi, lo] = sc[tab[T_COL + t]].reshape(4, 64, 128)

    def step_one(part, half):
        me, to = (z, to_z) if half == 0 else (y, to_y)
        waits = [
            send(s1.at[part, half, (me + d) % 4], mid.at[part, half, me], to(d), mid.at[part, half, (me + 4 - d) % 4])
            for d in RING
        ]
        return waits, local(s1.at[part, half, me], mid.at[part, half, me])

    def step_two(part, half, first):
        arrive(first[0])
        first[1].wait()
        me, to = (y, to_y) if half == 0 else (z, to_z)
        waits = [
            send(
                mid.at[part, half, :, (me + d) % 4], arr.at[part, half, me], to(d), arr.at[part, half, (me + 4 - d) % 4]
            )
            for d in RING
        ]
        copies.append(local(mid.at[part, half, :, me], arr.at[part, half, me]))
        return waits

    one, two = {}, []
    for part in range(4):
        if part == 0:
            arrive(a2)
            turn(0)
        if part == 2:
            arrive(b2)
            turn(1)
        arrive(child[part])
        for half in range(2):
            schur(part, half)
            one[part, half] = step_one(part, half)
        if part + 2 < 4:
            child[part + 2] = send_child(part + 2)
        if part >= 1:
            for half in range(2):
                two += step_two(part - 1, half, one[part - 1, half])
    for half in range(2):
        two += step_two(3, half, one[3, half])

    @pl.when(z == 0)
    def _():
        copy = pltpu.make_async_copy(front.at[:, 0], fp, lsem.at[N_SEMS - 1])
        copy.start()
        copy.wait()

    arrive(two)
    for copy in copies:
        copy.wait()
    keep = local(arr, arr_out)

    lanes = pl.ds(pl.multiple_of(y * 128, 128), 128)
    spread_sems = [sem() for _ in range(4)]

    def spread(d):
        n = spread_sems[d]
        return pltpu.make_async_remote_copy(
            extc.at[d], eq, ssem.at[n], rsem.at[n], device_id=(r, 4 * d + y), device_id_type=MESH
        )

    @pl.when(z == 0)
    def _():
        @pl.loop(0, 24)
        def _(i):
            added = fp[i].astype(F32) + arrived_tile(tab, arr, i, 0)
            extc[i // 6, (i % 6) // 2, i % 2] = added.astype(BF)

        for d in (1, 2, 3):
            spread(d).start()
        eq[...] = extc[0]
        for d in (1, 2, 3):
            spread(d).wait_send()

    for d in (1, 2, 3):

        @pl.when(z == d)
        def _():
            spread(d).wait_recv()

    e1 = [
        send(
            eq.at[:, :, pl.ds((y + d) % 4 * 32, 32)], ep.at[:, :, :, lanes], to_y(d),
            ep.at[:, :, :, pl.ds(pl.multiple_of((y + 4 - d) % 4 * 128, 128), 128)],
        )
        for d in RING
    ]
    local(eq.at[:, :, pl.ds(y * 32, 32)], ep.at[:, :, :, lanes]).wait()
    arrive(e1)
    made = jnp.dot(ep[...].reshape(192, 512), dinv[...], preferred_element_type=F32).astype(BF)
    y32 = pl.ds(y * 32, 32)
    prow[z, :, :, y32] = made.reshape(3, 2, 32, 512)
    p1 = [
        send(prow.at[z, :, 0, y32], prow.at[z, :, 0, y32], to_z(d), prow.at[(z + 4 - d) % 4, :, 0, y32]) for d in RING
    ]
    p2 = [
        send(prow.at[z, :, 1, y32], prow.at[z, :, 1, y32], to_y(d), prow.at[z, :, 1, pl.ds((y + 4 - d) % 4 * 32, 32)])
        for d in RING
    ]
    arrive(p1)
    p3 = [
        send(prow.at[:, :, 0, y32], prow.at[:, :, 0, y32], to_y(d), prow.at[:, :, 0, pl.ds((y + 4 - d) % 4 * 32, 32)])
        for d in RING
    ]
    arrive(p2)
    p4 = [send(prow.at[z, :, 1], prow.at[z, :, 1], to_z(d), prow.at[(z + 4 - d) % 4, :, 1]) for d in RING]
    arrive(p3)
    arrive(p4)

    root = c % 8
    upper = c // 8
    n_in = sem()
    n_out = [sem() for _ in ROWS]

    def piece(q):
        return pl.ds(q * 16, 16)

    def deal(dx, dk, n):
        q = row_dev(dx, dk)
        return pltpu.make_async_remote_copy(
            prow.at[:, :, upper, piece(q)], pcol.at[:, :, piece(q)], ssem.at[n], rsem.at[n_in],
            device_id=(q, c), device_id_type=MESH,
        )

    @pl.when(r == root)
    def _():
        for (dx, dk), n in zip(ROWS, n_out):
            deal(dx, dk, n).start()
        copy = pltpu.make_async_copy(prow.at[:, :, upper, piece(r)], pcol.at[:, :, piece(r)], lsem.at[N_SEMS - 2])
        copy.start()
        copy.wait()
        for (dx, dk), n in zip(ROWS, n_out):
            deal(dx, dk, n).wait_send()

    @pl.when(r != root)
    def _():
        pltpu.make_async_remote_copy(
            pcol.at[:, :, piece(r)], pcol.at[:, :, piece(r)], ssem.at[n_in], rsem.at[n_in],
            device_id=(r, c), device_id_type=MESH,
        ).wait_recv()

    q1 = [
        send(
            pcol.at[:, :, piece(r)], pcol.at[:, :, piece(r)], (row_dev(d, 0), c), pcol.at[:, :, piece(row_from(d, 0))]
        )
        for d in RING
    ]
    arrive(q1)
    q2 = [
        send(
            pcol.at[:, :, piece(2 * q + k)], pcol.at[:, :, piece(2 * q + k)], sibling,
            pcol.at[:, :, piece(2 * q + 1 - k)],
        )
        for q in range(4)
    ]
    arrive(q2)
    keep.wait()
    for copy in pending:
        copy.wait_send()


def update(tab, front, arr, prow, pcol, out, panel):
    r, c = lax.axis_index("row"), lax.axis_index("col")
    step = pl.program_id(0)
    rows = prow[...].reshape(256, 512)
    pick = (lax.broadcasted_iota(jnp.int32, (32, 512), 1) - 32 * c) == lax.broadcasted_iota(jnp.int32, (32, 512), 0)
    chosen = lax.dot_general(
        jnp.where(pick, 1.0, 0.0).astype(BF), rows, (((1,), (1,)), ((), ())), preferred_element_type=F32
    ).astype(BF)
    panel[0] = chosen[:, 0:128]
    panel[1] = chosen[:, 128:256]
    for n in range(6):
        first, second = 2 * n, 2 * n + 1
        right = jnp.concatenate([pcol[first // 3, first % 3], pcol[second // 3, second % 3]], axis=0)
        prod = lax.dot_general(rows, right, (((1,), (1,)), ((), ())), preferred_element_type=F32)
        for e in range(2):
            j = 2 * n + e
            for b in range(2):
                i = 2 * step + b
                ext = (front[b, j].astype(F32) + arrived_tile(tab, arr, i, j)).astype(BF)
                new = (ext.astype(F32) - prod[b * 128 : b * 128 + 128, e * 128 : e * 128 + 128]).astype(BF)
                trailing = jnp.logical_and(r + 8 * i >= 4, c + 16 * j >= 4)
                out[b, j] = jnp.where(trailing, new, ext)


def body(child_update, child_panel, front, diag_inverse, parent_tile):
    row, col = lax.axis_index("row"), lax.axis_index("col")
    tab = tables(parent_tile, row, col)
    u = child_update.reshape(16, 1024, 128)
    gt = child_panel.reshape(16, 128, 32).transpose(0, 2, 1)
    tiles = front.reshape(24, 128, 12, 128).transpose(0, 2, 1, 3)
    vmem, anywhere = pl.BlockSpec(memory_space=pltpu.VMEM), pl.BlockSpec(memory_space=pl.ANY)
    smem = pl.BlockSpec(memory_space=pltpu.SMEM)
    arr, prow, pcol = pl.pallas_call(
        exchange,
        out_shape=(
            jax.ShapeDtypeStruct((4, 2, 4, 4, 4, 64, 128), BF),
            jax.ShapeDtypeStruct((4, 3, 2, 128, 512), BF),
            jax.ShapeDtypeStruct((4, 3, 128, 512), BF),
        ),
        in_specs=[smem, vmem, vmem, anywhere, vmem],
        out_specs=(anywhere, vmem, vmem),
        scratch_shapes=[
            pltpu.VMEM((8, 2, 1024, 128), BF),
            pltpu.VMEM((8, 2, 1024, 128), BF),
            pltpu.VMEM((8, 4, 32, 128), BF),
            pltpu.VMEM((8, 4, 32, 128), BF),
            pltpu.VMEM((2, 8, 512, 128), BF),
            pltpu.VMEM((4, 8, 64, 512), BF),
            pltpu.VMEM((4, 4, 32, 128), BF),
            pltpu.VMEM((4, 4, 32, 128), BF),
            pltpu.VMEM((8, 4, 4, 32, 128), BF),
            pltpu.VMEM((512, 1024), BF),
            pltpu.VMEM((512, 1024), BF),
            pltpu.VMEM((2048, 128), F32),
            pltpu.VMEM((8, 256, 128), BF),
            pltpu.VMEM((4, 2, 4, 4, 4, 64, 128), BF),
            pltpu.VMEM((4, 2, 4, 4, 4, 64, 128), BF),
            pltpu.VMEM((4, 2, 4, 4, 4, 64, 128), BF),
            pltpu.VMEM((24, 128, 128), BF),
            pltpu.VMEM((4, 3, 2, 128, 128), BF),
            pltpu.VMEM((3, 2, 128, 128), BF),
            pltpu.VMEM((3, 2, 32, 512), BF),
            pltpu.SemaphoreType.DMA((N_SEMS,)),
            pltpu.SemaphoreType.DMA((N_SEMS,)),
            pltpu.SemaphoreType.DMA((N_SEMS,)),
        ],
        compiler_params=pltpu.CompilerParams(collective_id=0, has_side_effects=True, vmem_limit_bytes=60 << 20),
        name="exchange",
    )(tab, u, gt, tiles, diag_inverse)
    updated, panel = pl.pallas_call(
        update,
        grid_spec=pltpu.PrefetchScalarGridSpec(
            num_scalar_prefetch=1,
            grid=(12,),
            in_specs=[
                pl.BlockSpec((2, 12, 128, 128), lambda s, t: (s, 0, 0, 0)),
                pl.BlockSpec((4, 2, 4, 4, 4, 64, 128), lambda s, t: (0, 0, 0, 0, 0, 0, 0)),
                pl.BlockSpec((1, 1, 2, 128, 512), lambda s, t: (s // 3, s % 3, 0, 0, 0)),
                pl.BlockSpec((4, 3, 128, 512), lambda s, t: (0, 0, 0, 0)),
            ],
            out_specs=[
                pl.BlockSpec((2, 12, 128, 128), lambda s, t: (s, 0, 0, 0)),
                pl.BlockSpec((2, 32, 128), lambda s, t: (s, 0, 0)),
            ],
        ),
        out_shape=(jax.ShapeDtypeStruct((24, 12, 128, 128), BF), jax.ShapeDtypeStruct((24, 32, 128), BF)),
        compiler_params=pltpu.CompilerParams(vmem_limit_bytes=60 << 20),
        name="update",
    )(tab, tiles, arr, prow, pcol)
    return (
        panel.transpose(0, 2, 1).reshape(24, 1, 128, 1, 32),
        updated.transpose(0, 2, 1, 3).reshape(24, 1, 128, 12, 1, 128),
    )


def solution(mesh):
    return jax.shard_map(
        body,
        mesh=mesh,
        in_specs=(
            P(None, "row", None, None, "col", None),
            P(None, "row", None, "col"),
            P(None, "row", None, None, "col", None),
            P(),
            P(),
        ),
        out_specs=(P(None, "row", None, "col", None), P(None, "row", None, None, "col", None)),
        check_vma=False,
    )
```

```python
import jax
import jax.numpy as jnp
from jax import lax
from jax.experimental import pallas as pl
from jax.experimental.pallas import tpu as pltpu
from jax.sharding import PartitionSpec as P

MESH = pl.DeviceIdType.MESH
BF = jnp.bfloat16
F32 = jnp.float32
ROWS = [(1, 0), (3, 0), (1, 1), (3, 1), (2, 0), (2, 1), (0, 1)]
RING = [1, 3, 2]
N_SEMS = 256
KERNEL_VMEM = 46 << 20


def tables(parent_tile, row, col):
    ids = jnp.arange(128, dtype=jnp.int32)
    same = ((ids[:, None] - ids[None, :]) % 8 == 0) & ((parent_tile[:, None] - parent_tile[None, :]) % 8 == 0)
    rank = jnp.any(same & (ids[None, :] < ids[:, None]), axis=1).astype(jnp.int32)[None, :]
    e = jnp.arange(128, dtype=jnp.int32)[:, None]
    a, to = ids[None, :], parent_tile[None, :]
    sent_row = (a % 8 == row) & (to % 8 == e // 2) & (rank == e % 2)
    sent_col = (a % 16 == col) & (to % 16 == e - T_COL)
    got_row = to == row + 8 * ((e - T_RFROM) % 24)
    got_col = to == col + 16 * ((e - T_CFROM) % 12)
    hit = jnp.where(e < T_COL, sent_row, jnp.where(e < T_RFROM, sent_col, jnp.where(e < T_CFROM, got_row, got_col)))
    got_panel = (a % 16 == col) & (to == (e - T_PFROM) % 4)
    hit = jnp.where(e < T_PFROM, hit, got_panel)
    row_value = jnp.where(e < T_ROK, rank * 8 + a % 8, 1)
    col_value = jnp.where(e < T_COK, a % 16, 1)
    value = jnp.where(
        e < T_COL, a // 8, jnp.where(e < T_RFROM, a // 16, jnp.where(e < T_CFROM, row_value, col_value))
    )
    value = jnp.where(e < T_PFROM, value, jnp.where(e < T_POK, a // 16, 1))
    return jnp.sum(jnp.where(hit, value, 0), axis=1)


T_COL, T_RFROM, T_ROK, T_CFROM, T_COK, T_PFROM, T_POK = 16, 32, 56, 80, 92, 104, 108


def arrived_place(tab, i, j):
    source_row, source = tab[T_RFROM + i], tab[T_CFROM + j]
    half = source_row % 8 // 4
    major = jnp.where(half == 0, source % 4, source // 4)
    minor = jnp.where(half == 0, source // 4, source % 4)
    return source_row // 8, half, source_row % 4, major, minor, (tab[T_ROK + i] * tab[T_COK + j]) == 1


def exchange(
    tab, u, gt, front, dinv, arr, prow, pcol,
    us, ux, g1s, g1r, rowg, rowt, cmid, colt, colgr, colga, colgb, uf, sc, s1, mid, pst, psp, ra, sa, ra2, rb, sb, rb2,
    eq, fe, pp, lsem, ssem, rsem,
):
    r, c = lax.axis_index("row"), lax.axis_index("col")
    x, k, z, y = r // 2, r % 2, c // 4, c % 4
    counter = [0]
    pending = []

    def row_dev(dx, dk):
        return ((x + dx) % 4) * 2 + (k + dk) % 2

    def row_from(dx, dk):
        return ((x + 4 - dx) % 4) * 2 + (k + dk) % 2

    def sem(count=1):
        counter[0] += count
        return counter[0] - count

    def remote(src, dst, n_send, n_recv, dev):
        return pltpu.make_async_remote_copy(
            src, dst, ssem.at[n_send], rsem.at[n_recv], device_id=dev, device_id_type=MESH
        )

    def send(src, dst, dev, landing):
        n = sem()
        out = remote(src, dst, n, n, dev)
        out.start()
        pending.append(out)
        return remote(landing, landing, n, n, dev)

    def arrive(waits):
        for w in waits:
            w.wait_recv()

    def local(src, dst):
        n = sem()
        copy = pltpu.make_async_copy(src, dst, lsem.at[n])
        copy.start()
        return copy

    def at_z(n):
        return (r, n * 4 + y)

    def to_z(d):
        return at_z((z + d) % 4)

    def to_y(d):
        return (r, z * 4 + (y + d) % 4)

    load = local(u, s1.at[0:2])
    for rp in range(8):
        g1s[rp, 0] = gt[tab[2 * rp]]
        g1s[rp, 1] = gt[tab[2 * rp + 1]]
        g1s[rp, 2] = gt[2 * rp]
        g1s[rp, 3] = gt[2 * rp + 1]

    barrier = pltpu.get_barrier_semaphore()
    for dx, dk in ROWS:
        pl.semaphore_signal(barrier, inc=1, device_id=(row_dev(dx, dk), c), device_id_type=MESH)
    for d in RING:
        pl.semaphore_signal(barrier, inc=1, device_id=to_z(d), device_id_type=MESH)
        pl.semaphore_signal(barrier, inc=1, device_id=to_y(d), device_id_type=MESH)
    pl.semaphore_wait(barrier, 13)

    g1 = [
        send(g1s.at[row_dev(dx, dk)], g1r.at[r], (row_dev(dx, dk), c), g1r.at[row_from(dx, dk)])
        for dx, dk in ROWS
    ]
    g1r[r] = g1s[r]
    def send_child(part, which=ROWS):
        rank, rows = part // 2, pl.ds((part % 2) * 512, 512)
        return [
            send(
                us.at[row_dev(dx, dk), rank, rows], ux.at[r, rank, rows], (row_dev(dx, dk), c),
                ux.at[row_from(dx, dk), rank, rows],
            )
            for dx, dk in which
        ]

    spread_sems = sem(4)

    def spread(d):
        return remote(front.at[d, :, :, 0], eq, spread_sems + d, spread_sems + d, at_z(d))

    arrive(g1)
    yz, zy = pl.ds((y * 4 + z) * 32, 32), pl.ds((z * 4 + y) * 32, 32)
    y128, z128 = pl.ds(y * 128, 128), pl.ds(z * 128, 128)

    def col_piece(zp):
        return g1r.at[pl.ds(4 * (zp % 2), 4), 2 + zp // 2]

    def rows_one(rank):
        top, low = rowg.at[rank, 0:4], rowg.at[rank, 4:8]
        waits_a, waits_b = [], []
        for d in RING:
            got = pl.ds((y * 4 + (z + 4 - d) % 4) * 32, 32)
            waits_a.append(send(g1r.at[0:4, rank], top.at[:, yz], to_z(d), top.at[:, got]))
            got = pl.ds((z * 4 + (y + 4 - d) % 4) * 32, 32)
            waits_b.append(send(g1r.at[4:8, rank], low.at[:, zy], to_y(d), low.at[:, got]))
        own = [local(g1r.at[0:4, rank], top.at[:, yz]), local(g1r.at[4:8, rank], low.at[:, zy])]
        return waits_a, waits_b, own

    def rows_two(rank, first):
        top, low = rowg.at[rank, 0:4], rowg.at[rank, 4:8]
        for copy in first[2]:
            copy.wait()
        waits = []
        arrive(first[0])
        for d in RING:
            got = pl.ds((y + 4 - d) % 4 * 128, 128)
            waits.append(send(top.at[:, y128], top.at[:, y128], to_y(d), top.at[:, got]))
        arrive(first[1])
        for d in RING:
            got = pl.ds((z + 4 - d) % 4 * 128, 128)
            waits.append(send(low.at[:, z128], low.at[:, z128], to_z(d), low.at[:, got]))
        return waits

    c1 = [send(col_piece((z + d) % 4), cmid.at[z], to_z(d), cmid.at[(z + 4 - d) % 4]) for d in RING]
    own = local(col_piece(z), cmid.at[z])
    g0 = rows_one(0)
    load.wait()

    @pl.loop(0, 16)
    def _(n):
        t = tab[n]
        us[n // 2, n % 2] = s1[t // 8, t // 4 % 2, t % 4].reshape(1024, 128)

    child = {0: send_child(0, ROWS[:4])}
    ux[r] = us[r]
    own.wait()
    arrive(c1)
    c2 = [send(cmid.at[:, (y + d) % 4], colt.at[y], to_y(d), colt.at[(y + 4 - d) % 4]) for d in RING]
    mine = local(cmid.at[:, y], colt.at[y])
    g0 = rows_two(0, g0)
    child[0] += send_child(0, ROWS[4:])
    g1 = rows_one(1)
    mine.wait()
    arrive(c2)
    d1 = [send(colt, colgr.at[r], (row_dev(d, 0), c), colgr.at[row_from(d, 0)]) for d in RING]
    local(colt, colgr.at[r]).wait()
    arrive(d1)
    sibling = (row_dev(0, 1), c)
    d2 = [send(colgr.at[2 * q + k], colgr.at[2 * q + k], sibling, colgr.at[2 * q + 1 - k]) for q in range(4)]
    g1 = rows_two(1, g1)
    child[1] = send_child(1)
    arrive(d2)

    @pl.when(z == 0)
    def _():
        for d in (1, 2, 3):
            spread(d).start()
        copy = pltpu.make_async_copy(front.at[0, :, :, 0], eq, lsem.at[N_SEMS - 1])
        copy.start()
        copy.wait()

    for j in range(8):
        for a in range(4):
            for b in range(4):
                piece = colgr[j, a, b]
                colga[pl.ds((a * 4 + b) * 32, 32), pl.ds(j * 128, 128)] = piece
                colgb[pl.ds((b * 4 + a) * 32, 32), pl.ds(j * 128, 128)] = piece

    def turn(rank):
        @pl.loop(0, 8)
        def _(q):
            turned = rowg[rank, q].T
            rowt[2 * rank, q] = turned[0:64]
            rowt[2 * rank + 1, q] = turned[64:128]

    def schur(part, half):
        rank = part // 2
        colg = colga if half == 0 else colgb

        @pl.loop(0, 4)
        def _(q):
            uf[pl.ds(q * 512, 512)] = ux[half * 4 + q, rank, pl.ds((part % 2) * 512, 512)].astype(F32)

        left = rowt.at[part, pl.ds(half * 4, 4)]

        for n in range(4):
            prod = jnp.dot(
                left[...].reshape(256, 512), colg[:, n * 256 : n * 256 + 256], preferred_element_type=F32
            )
            for e in range(2):
                j = 2 * n + e
                sc[j] = (uf[pl.ds(j, 256, stride=8), :] - prod[:, e * 128 : e * 128 + 128]).astype(BF)

        @pl.loop(0, 16)
        def _(t):
            lo, hi = t // 4, t % 4
            if half == 0:
                s1[part, half, lo, hi] = sc[tab[T_COL + t]]
            else:
                s1[part, half, hi, lo] = sc[tab[T_COL + t]]

        for t in range(4):
            tile = sc[tab[T_PFROM + t]]
            tile = jnp.where(tab[T_POK + t] == 1, tile, jnp.zeros_like(tile)).reshape(4, 64, 128)
            pst[part, half, :, :, t * 128 : t * 128 + 128] = tile

    copies = []

    def step_one(part):
        for half in range(2):
            one[part, half] = step_half(part, half)

    def step_half(part, half):
        me, to = (z, to_z) if half == 0 else (y, to_y)
        waits = [
            send(s1.at[part, half, (me + d) % 4], mid.at[part, half, me], to(d), mid.at[part, half, (me + 4 - d) % 4])
            for d in RING
        ]
        return waits, local(s1.at[part, half, me], mid.at[part, half, me])

    def step_two(part):
        for half in range(2):
            arrive(one[part, half][0])
            one[part, half][1].wait()
            me, to = (y, to_y) if half == 0 else (z, to_z)
            for d in RING:
                two.append(
                    send(
                        mid.at[part, half, :, (me + d) % 4], arr.at[part, half, me], to(d),
                        arr.at[part, half, (me + 4 - d) % 4],
                    )
                )
            copies.append(local(mid.at[part, half, :, me], arr.at[part, half, me]))

    one, two = {}, []

    def make(part):
        if part % 2 == 0:
            arrive(g0 if part == 0 else g1)
            turn(part // 2)
        arrive(child[part])
        for half in range(2):
            schur(part, half)
        if part + 2 < 4:
            child[part + 2] = send_child(part + 2)

    make(0)
    step_one(0)
    lanes = pl.ds(pl.multiple_of(y * 128, 128), 128)
    for d in (1, 2, 3):

        @pl.when(z == 0)
        def _():
            spread(d).wait_send()

        @pl.when(z == d)
        def _():
            spread(d).wait_recv()

    e1 = [
        send(
            eq.at[:, :, pl.ds((y + d) % 4 * 32, 32)], fe.at[:, :, :, lanes], to_y(d),
            fe.at[:, :, :, pl.ds(pl.multiple_of((y + 4 - d) % 4 * 128, 128), 128)],
        )
        for d in RING
    ]
    copies.append(local(eq.at[:, :, pl.ds(y * 32, 32)], fe.at[:, :, :, lanes]))
    make(1)
    step_one(1)
    step_two(0)
    make(2)
    make(3)

    @pl.loop(0, 24)
    def _(i):
        source_row = tab[T_RFROM + i]
        rank, half = source_row // 8, source_row % 8 // 4
        place = source_row % 4
        tile = jnp.concatenate([pst[rank * 2, half, place], pst[rank * 2 + 1, half, place]], axis=0)
        psp[i // 6, i % 6 // 2, i % 2] = jnp.where(tab[T_ROK + i] == 1, tile, jnp.zeros_like(tile))

    y32 = pl.ds(pl.multiple_of(y * 32, 32), 32)
    f1, f2 = [], []
    for n, d in enumerate(RING):
        f1.append(send(psp.at[(z + d) % 4, :, 0], ra.at[n], to_z(d), ra.at[n]))
        f2.append(send(psp.at[:, :, 1, pl.ds((y + d) % 4 * 32, 32)], rb.at[n], to_y(d), rb.at[n]))
    step_two(1)
    arrive(f1)
    sa[...] = psp[z, :, 0] + ra[0] + ra[1] + ra[2]
    f3 = [send(sa.at[:, pl.ds((y + d) % 4 * 32, 32)], ra2.at[n], to_y(d), ra2.at[n]) for n, d in enumerate(RING)]
    arrive(f2)
    sb[...] = psp[:, :, 1, y32] + rb[0] + rb[1] + rb[2]
    f4 = [send(sb.at[(z + d) % 4], rb2.at[n], to_z(d), rb2.at[n]) for n, d in enumerate(RING)]
    step_one(2)
    arrive(f3)
    arrive(f4)
    arrive(e1)
    copies[0].wait()
    even = sa[:, y32] + ra2[0] + ra2[1] + ra2[2]
    odd = sb[z] + rb2[0] + rb2[1] + rb2[2]
    even = (fe[:, 0].astype(F32) + even.astype(F32)).astype(BF).reshape(96, 512)
    odd = (fe[:, 1].astype(F32) + odd.astype(F32)).astype(BF).reshape(96, 512)
    pp[:, 0] = jnp.dot(even, dinv[...], preferred_element_type=F32).astype(BF).reshape(3, 32, 512)
    pp[:, 1] = jnp.dot(odd, dinv[...], preferred_element_type=F32).astype(BF).reshape(3, 32, 512)
    own = local(pp, prow.at[z, :, :, y32])
    p1, p2 = [], []
    for d in RING:
        p1.append(send(pp.at[:, 0], prow.at[z, :, 0, y32], to_z(d), prow.at[(z + 4 - d) % 4, :, 0, y32]))
        p2.append(send(pp.at[:, 1], prow.at[z, :, 1, y32], to_y(d), prow.at[z, :, 1, pl.ds((y + 4 - d) % 4 * 32, 32)]))
    own.wait()
    step_one(3)
    arrive(p1)
    p3 = [
        send(prow.at[:, :, 0, y32], prow.at[:, :, 0, y32], to_y(d), prow.at[:, :, 0, pl.ds((y + 4 - d) % 4 * 32, 32)])
        for d in RING
    ]
    arrive(p2)
    p4 = [send(prow.at[z, :, 1], prow.at[z, :, 1], to_z(d), prow.at[(z + 4 - d) % 4, :, 1]) for d in RING]
    step_two(2)
    arrive(p3)
    arrive(p4)

    root = c % 8
    upper = c // 8
    n_in = sem()
    n_out = [sem() for _ in ROWS]

    def piece(q):
        return pl.ds(q * 16, 16)

    def deal(dx, dk, n):
        q = row_dev(dx, dk)
        return remote(prow.at[:, :, upper, piece(q)], pcol.at[:, :, piece(q)], n, n_in, (q, c))

    @pl.when(r == root)
    def _():
        for (dx, dk), n in zip(ROWS, n_out):
            deal(dx, dk, n).start()
        copy = pltpu.make_async_copy(prow.at[:, :, upper, piece(r)], pcol.at[:, :, piece(r)], lsem.at[N_SEMS - 2])
        copy.start()
        copy.wait()
        for (dx, dk), n in zip(ROWS, n_out):
            deal(dx, dk, n).wait_send()

    @pl.when(r != root)
    def _():
        remote(pcol.at[:, :, piece(r)], pcol.at[:, :, piece(r)], n_in, n_in, (r, c)).wait_recv()

    q1 = [
        send(
            pcol.at[:, :, piece(r)], pcol.at[:, :, piece(r)], (row_dev(d, 0), c), pcol.at[:, :, piece(row_from(d, 0))]
        )
        for d in RING
    ]
    step_two(3)
    arrive(q1)
    q2 = [
        send(
            pcol.at[:, :, piece(2 * q + k)], pcol.at[:, :, piece(2 * q + k)], sibling,
            pcol.at[:, :, piece(2 * q + 1 - k)],
        )
        for q in range(4)
    ]

    arrive(q2)
    arrive(two)
    for copy in copies[1:]:
        copy.wait()
    for copy in pending:
        copy.wait_send()


def update(tab, front, *refs):
    arrs, (prow, pcol, out, panel, right) = refs[:4], refs[4:]
    r, c = lax.axis_index("row"), lax.axis_index("col")
    step = pl.program_id(0)

    @pl.when(step == 0)
    def _():
        for j in range(12):
            tile = pcol[j // 3, j % 3]
            if j == 0:
                tile = jnp.where(c >= 4, tile, jnp.zeros_like(tile))
            right[:, j * 128 : j * 128 + 128] = tile.T

    rows = prow[...].reshape(256, 512)
    pick = (lax.broadcasted_iota(jnp.int32, (32, 512), 1) - 32 * c) == lax.broadcasted_iota(jnp.int32, (32, 512), 0)
    chosen = lax.dot_general(
        jnp.where(pick, 1.0, 0.0).astype(BF), rows, (((1,), (1,)), ((), ())), preferred_element_type=F32
    ).astype(BF)
    panel[0] = chosen[:, 0:128]
    panel[1] = chosen[:, 128:256]
    trailing = jnp.logical_or(step > 0, r >= 4)
    rows = jnp.concatenate([jnp.where(trailing, rows[0:128], jnp.zeros_like(rows[0:128])), rows[128:256]], axis=0)
    for n in range(6):
        prod = jnp.dot(rows, right[:, n * 256 : n * 256 + 256], preferred_element_type=F32)
        for e in range(2):
            for b in range(2):
                j = 2 * n + e
                _, _, _, major, minor, ok = arrived_place(tab, 2 * step + b, j)
                for p in range(2):
                    tile = arrs[2 * b + p][0, 0, major, minor]
                    lines = slice(p * 64, p * 64 + 64)
                    ext = (
                        front[b, j, lines].astype(F32) + jnp.where(ok, tile, jnp.zeros_like(tile)).astype(F32)
                    ).astype(BF)
                    term = prod[b * 128 + p * 64 : b * 128 + p * 64 + 64, e * 128 : e * 128 + 128]
                    out[b, j, lines] = (ext.astype(F32) - term).astype(BF)


def arrivals(b, p):
    def index(step, tab):
        source_row = tab[T_RFROM + 2 * step + b]
        return (source_row // 8 * 2 + p, source_row % 8 // 4, 0, 0, source_row % 4, 0)

    return pl.BlockSpec((1, 1, 4, 4, 64, 128), index)


def body(child_update, child_panel, front, diag_inverse, parent_tile):
    tab = tables(parent_tile, lax.axis_index("row"), lax.axis_index("col"))
    u = child_update.reshape(2, 2, 4, 4, 256, 128)
    gt = child_panel.reshape(16, 128, 32).transpose(0, 2, 1)
    tiles = front.reshape(24, 128, 12, 128).transpose(0, 2, 1, 3)
    vmem, anywhere = pl.BlockSpec(memory_space=pltpu.VMEM), pl.BlockSpec(memory_space=pl.ANY)
    smem = pl.BlockSpec(memory_space=pltpu.SMEM)
    arr, prow, pcol = pl.pallas_call(
        exchange,
        out_shape=(
            jax.ShapeDtypeStruct((4, 2, 4, 4, 256, 128), BF),
            jax.ShapeDtypeStruct((4, 3, 2, 128, 512), BF),
            jax.ShapeDtypeStruct((4, 3, 128, 512), BF),
        ),
        in_specs=[smem, anywhere, vmem, anywhere, vmem],
        out_specs=(anywhere, anywhere, anywhere),
        scratch_shapes=[
            pltpu.VMEM((8, 2, 1024, 128), BF),
            pltpu.VMEM((8, 2, 1024, 128), BF),
            pltpu.VMEM((8, 4, 32, 128), BF),
            pltpu.VMEM((8, 4, 32, 128), BF),
            pltpu.VMEM((2, 8, 512, 128), BF),
            pltpu.VMEM((4, 8, 64, 512), BF),
            pltpu.VMEM((4, 4, 32, 128), BF),
            pltpu.VMEM((4, 4, 32, 128), BF),
            pltpu.VMEM((8, 4, 4, 32, 128), BF),
            pltpu.VMEM((512, 1024), BF),
            pltpu.VMEM((512, 1024), BF),
            pltpu.VMEM((2048, 128), F32),
            pltpu.VMEM((8, 256, 128), BF),
            pltpu.VMEM((4, 2, 4, 4, 256, 128), BF),
            pltpu.VMEM((4, 2, 4, 4, 256, 128), BF),
            pltpu.VMEM((4, 2, 4, 64, 512), BF),
            pltpu.VMEM((4, 3, 2, 128, 512), BF),
            pltpu.VMEM((3, 3, 128, 512), BF),
            pltpu.VMEM((3, 128, 512), BF),
            pltpu.VMEM((3, 3, 32, 512), BF),
            pltpu.VMEM((3, 4, 3, 32, 512), BF),
            pltpu.VMEM((4, 3, 32, 512), BF),
            pltpu.VMEM((3, 3, 32, 512), BF),
            pltpu.VMEM((3, 2, 128, 128), BF),
            pltpu.VMEM((3, 2, 32, 512), BF),
            pltpu.VMEM((3, 2, 32, 512), BF),
            pltpu.SemaphoreType.DMA((N_SEMS,)),
            pltpu.SemaphoreType.DMA((N_SEMS,)),
            pltpu.SemaphoreType.DMA((N_SEMS,)),
        ],
        compiler_params=pltpu.CompilerParams(collective_id=0, has_side_effects=True, vmem_limit_bytes=KERNEL_VMEM),
        name="exchange",
    )(tab, u, gt, tiles.reshape(4, 3, 2, 12, 128, 128), diag_inverse)
    updated, panel = pl.pallas_call(
        update,
        grid_spec=pltpu.PrefetchScalarGridSpec(
            num_scalar_prefetch=1,
            grid=(12,),
            in_specs=[
                pl.BlockSpec((2, 12, 128, 128), lambda s, t: (s, 0, 0, 0)),
                arrivals(0, 0),
                arrivals(0, 1),
                arrivals(1, 0),
                arrivals(1, 1),
                pl.BlockSpec((1, 1, 2, 128, 512), lambda s, t: (s // 3, s % 3, 0, 0, 0)),
                pl.BlockSpec((4, 3, 128, 512), lambda s, t: (0, 0, 0, 0)),
            ],
            out_specs=[
                pl.BlockSpec((2, 12, 128, 128), lambda s, t: (s, 0, 0, 0)),
                pl.BlockSpec((2, 32, 128), lambda s, t: (s, 0, 0)),
            ],
            scratch_shapes=[pltpu.VMEM((512, 1536), BF)],
        ),
        out_shape=(jax.ShapeDtypeStruct((24, 12, 128, 128), BF), jax.ShapeDtypeStruct((24, 32, 128), BF)),
        compiler_params=pltpu.CompilerParams(vmem_limit_bytes=46 << 20),
        name="update",
    )(tab, tiles, arr, arr, arr, arr, prow, pcol)
    return (
        panel.transpose(0, 2, 1).reshape(24, 1, 128, 1, 32),
        updated.transpose(0, 2, 1, 3).reshape(24, 1, 128, 12, 1, 128),
    )


def solution(mesh):
    return jax.shard_map(
        body,
        mesh=mesh,
        in_specs=(
            P(None, "row", None, None, "col", None),
            P(None, "row", None, "col"),
            P(None, "row", None, None, "col", None),
            P(),
            P(),
        ),
        out_specs=(P(None, "row", None, "col", None), P(None, "row", None, None, "col", None)),
        check_vma=False,
    )
```

```python
import jax
import jax.numpy as jnp
from jax import lax
from jax.experimental import pallas as pl
from jax.experimental.pallas import tpu as pltpu
from jax.sharding import PartitionSpec as P

MESH = pl.DeviceIdType.MESH
BF = jnp.bfloat16
F32 = jnp.float32
ROWS = [(1, 0), (3, 0), (1, 1), (3, 1), (2, 0), (2, 1), (0, 1)]
RING = [1, 3, 2]
N_SEMS = 256
KERNEL_VMEM = 46 << 20


def tables(parent_tile, row, col):
    ids = jnp.arange(128, dtype=jnp.int32)
    same = ((ids[:, None] - ids[None, :]) % 8 == 0) & ((parent_tile[:, None] - parent_tile[None, :]) % 8 == 0)
    rank = jnp.any(same & (ids[None, :] < ids[:, None]), axis=1).astype(jnp.int32)[None, :]
    e = jnp.arange(128, dtype=jnp.int32)[:, None]
    a, to = ids[None, :], parent_tile[None, :]
    sent_row = (a % 8 == row) & (to % 8 == e // 2) & (rank == e % 2)
    sent_col = (a % 16 == col) & (to % 16 == e - T_COL)
    got_row = to == row + 8 * ((e - T_RFROM) % 24)
    got_col = to == col + 16 * ((e - T_CFROM) % 12)
    hit = jnp.where(e < T_COL, sent_row, jnp.where(e < T_RFROM, sent_col, jnp.where(e < T_CFROM, got_row, got_col)))
    got_panel = (a % 16 == col) & (to == (e - T_PFROM) % 4)
    hit = jnp.where(e < T_PFROM, hit, got_panel)
    row_value = jnp.where(e < T_ROK, rank * 8 + a % 8, 1)
    col_value = jnp.where(e < T_COK, a % 16, 1)
    value = jnp.where(
        e < T_COL, a // 8, jnp.where(e < T_RFROM, a // 16, jnp.where(e < T_CFROM, row_value, col_value))
    )
    value = jnp.where(e < T_PFROM, value, jnp.where(e < T_POK, a // 16, 1))
    return jnp.sum(jnp.where(hit, value, 0), axis=1)


T_COL, T_RFROM, T_ROK, T_CFROM, T_COK, T_PFROM, T_POK = 16, 32, 56, 80, 92, 104, 108


def arrived_place(tab, i, j):
    source_row, source = tab[T_RFROM + i], tab[T_CFROM + j]
    half = source_row % 8 // 4
    major = jnp.where(half == 0, source % 4, source // 4)
    minor = jnp.where(half == 0, source // 4, source % 4)
    return source_row // 8, half, source_row % 4, major, minor, (tab[T_ROK + i] * tab[T_COK + j]) == 1


def exchange(
    tab, u, gt, front, dinv, arr, prow, pcol,
    us, ux, g1s, g1r, rowg, rowt, cmid, colt, colgr, colga, colgb, uf, sc, s1, mid, pst, psp, ra, sa, ra2, rb, sb, rb2,
    eq, fe, pp, lsem, ssem, rsem,
):
    r, c = lax.axis_index("row"), lax.axis_index("col")
    x, k, z, y = r // 2, r % 2, c // 4, c % 4
    counter = [0]
    pending = []

    def row_dev(dx, dk):
        return ((x + dx) % 4) * 2 + (k + dk) % 2

    def row_from(dx, dk):
        return ((x + 4 - dx) % 4) * 2 + (k + dk) % 2

    def sem(count=1):
        counter[0] += count
        return counter[0] - count

    def remote(src, dst, n_send, n_recv, dev):
        return pltpu.make_async_remote_copy(
            src, dst, ssem.at[n_send], rsem.at[n_recv], device_id=dev, device_id_type=MESH
        )

    def send(src, dst, dev, landing):
        n = sem()
        out = remote(src, dst, n, n, dev)
        out.start()
        pending.append(out)
        return remote(landing, landing, n, n, dev)

    def arrive(waits):
        for w in waits:
            w.wait_recv()

    def local(src, dst):
        n = sem()
        copy = pltpu.make_async_copy(src, dst, lsem.at[n])
        copy.start()
        return copy

    def at_z(n):
        return (r, n * 4 + y)

    def to_z(d):
        return at_z((z + d) % 4)

    def to_y(d):
        return (r, z * 4 + (y + d) % 4)

    load = local(u, s1.at[0:2])
    for rp in range(8):
        g1s[rp, 0] = gt[tab[2 * rp]]
        g1s[rp, 1] = gt[tab[2 * rp + 1]]
        g1s[rp, 2] = gt[2 * rp]
        g1s[rp, 3] = gt[2 * rp + 1]

    barrier = pltpu.get_barrier_semaphore()
    for dx, dk in ROWS:
        pl.semaphore_signal(barrier, inc=1, device_id=(row_dev(dx, dk), c), device_id_type=MESH)
    for d in RING:
        pl.semaphore_signal(barrier, inc=1, device_id=to_z(d), device_id_type=MESH)
        pl.semaphore_signal(barrier, inc=1, device_id=to_y(d), device_id_type=MESH)
    pl.semaphore_wait(barrier, 13)

    g1 = [
        send(g1s.at[row_dev(dx, dk)], g1r.at[r], (row_dev(dx, dk), c), g1r.at[row_from(dx, dk)])
        for dx, dk in ROWS
    ]
    g1r[r] = g1s[r]

    spread_sems = sem(4)

    def spread(d):
        return remote(front.at[d, :, :, 0], eq, spread_sems + d, spread_sems + d, at_z(d))

    @pl.when(z == 0)
    def _():
        for d in (1, 2, 3):
            spread(d).start()
        copy = pltpu.make_async_copy(front.at[0, :, :, 0], eq, lsem.at[N_SEMS - 1])
        copy.start()
    def send_child(part, which=ROWS):
        rank, rows = part // 2, pl.ds((part % 2) * 512, 512)
        return [
            send(
                us.at[row_dev(dx, dk), rank, rows], ux.at[r, rank, rows], (row_dev(dx, dk), c),
                ux.at[row_from(dx, dk), rank, rows],
            )
            for dx, dk in which
        ]

    arrive(g1)
    yz, zy = pl.ds((y * 4 + z) * 32, 32), pl.ds((z * 4 + y) * 32, 32)
    y128, z128 = pl.ds(y * 128, 128), pl.ds(z * 128, 128)

    def col_piece(zp):
        return g1r.at[pl.ds(4 * (zp % 2), 4), 2 + zp // 2]

    def rows_one(rank):
        top, low = rowg.at[rank, 0:4], rowg.at[rank, 4:8]
        waits_a, waits_b = [], []
        for d in RING:
            got = pl.ds((y * 4 + (z + 4 - d) % 4) * 32, 32)
            waits_a.append(send(g1r.at[0:4, rank], top.at[:, yz], to_z(d), top.at[:, got]))
            got = pl.ds((z * 4 + (y + 4 - d) % 4) * 32, 32)
            waits_b.append(send(g1r.at[4:8, rank], low.at[:, zy], to_y(d), low.at[:, got]))
        own = [local(g1r.at[0:4, rank], top.at[:, yz]), local(g1r.at[4:8, rank], low.at[:, zy])]
        return waits_a, waits_b, own

    def rows_two(rank, first):
        top, low = rowg.at[rank, 0:4], rowg.at[rank, 4:8]
        for copy in first[2]:
            copy.wait()
        waits = []
        arrive(first[0])
        for d in RING:
            got = pl.ds((y + 4 - d) % 4 * 128, 128)
            waits.append(send(top.at[:, y128], top.at[:, y128], to_y(d), top.at[:, got]))
        arrive(first[1])
        for d in RING:
            got = pl.ds((z + 4 - d) % 4 * 128, 128)
            waits.append(send(low.at[:, z128], low.at[:, z128], to_z(d), low.at[:, got]))
        return waits

    c1 = [send(col_piece((z + d) % 4), cmid.at[z], to_z(d), cmid.at[(z + 4 - d) % 4]) for d in RING]
    own = local(col_piece(z), cmid.at[z])
    g0 = rows_one(0)
    load.wait()

    @pl.loop(0, 16)
    def _(n):
        t = tab[n]
        us[n // 2, n % 2] = s1[t // 8, t // 4 % 2, t % 4].reshape(1024, 128)

    child = {0: send_child(0, ROWS[:4])}
    ux[r] = us[r]
    own.wait()
    arrive(c1)
    c2 = [send(cmid.at[:, (y + d) % 4], colt.at[y], to_y(d), colt.at[(y + 4 - d) % 4]) for d in RING]
    mine = local(cmid.at[:, y], colt.at[y])
    g0 = rows_two(0, g0)
    child[0] += send_child(0, ROWS[4:])
    g1 = rows_one(1)
    mine.wait()
    arrive(c2)
    d1 = [send(colt, colgr.at[r], (row_dev(d, 0), c), colgr.at[row_from(d, 0)]) for d in RING]
    lanes = pl.ds(pl.multiple_of(y * 128, 128), 128)
    for d in (1, 2, 3):

        @pl.when(z == 0)
        def _():
            spread(d).wait_send()
            if d == 1:
                pltpu.make_async_copy(front.at[0, :, :, 0], eq, lsem.at[N_SEMS - 1]).wait()

        @pl.when(z == d)
        def _():
            spread(d).wait_recv()

    e1 = [
        send(
            eq.at[:, :, pl.ds((y + d) % 4 * 32, 32)], fe.at[:, :, :, lanes], to_y(d),
            fe.at[:, :, :, pl.ds(pl.multiple_of((y + 4 - d) % 4 * 128, 128), 128)],
        )
        for d in RING
    ]
    own_fe = local(eq.at[:, :, pl.ds(y * 32, 32)], fe.at[:, :, :, lanes])
    local(colt, colgr.at[r]).wait()
    arrive(d1)
    sibling = (row_dev(0, 1), c)
    d2 = [send(colgr.at[2 * q + k], colgr.at[2 * q + k], sibling, colgr.at[2 * q + 1 - k]) for q in range(4)]
    child[1] = send_child(1)
    arrive(d2)

    for j in range(8):
        for a in range(4):
            for b in range(4):
                piece = colgr[j, a, b]
                colga[pl.ds((a * 4 + b) * 32, 32), pl.ds(j * 128, 128)] = piece
                colgb[pl.ds((b * 4 + a) * 32, 32), pl.ds(j * 128, 128)] = piece

    def turn(rank):
        @pl.loop(0, 8)
        def _(q):
            turned = rowg[rank, q].T
            rowt[2 * rank, q] = turned[0:64]
            rowt[2 * rank + 1, q] = turned[64:128]

    def schur(part, half):
        rank = part // 2
        colg = colga if half == 0 else colgb

        @pl.loop(0, 4)
        def _(q):
            uf[pl.ds(q * 512, 512)] = ux[half * 4 + q, rank, pl.ds((part % 2) * 512, 512)].astype(F32)

        left = rowt.at[part, pl.ds(half * 4, 4)]

        for n in range(4):
            prod = jnp.dot(
                left[...].reshape(256, 512), colg[:, n * 256 : n * 256 + 256], preferred_element_type=F32
            )
            for e in range(2):
                j = 2 * n + e
                sc[j] = (uf[pl.ds(j, 256, stride=8), :] - prod[:, e * 128 : e * 128 + 128]).astype(BF)

        @pl.loop(0, 16)
        def _(t):
            lo, hi = t // 4, t % 4
            if half == 0:
                s1[part, half, lo, hi] = sc[tab[T_COL + t]]
            else:
                s1[part, half, hi, lo] = sc[tab[T_COL + t]]

        for t in range(4):
            tile = sc[tab[T_PFROM + t]]
            tile = jnp.where(tab[T_POK + t] == 1, tile, jnp.zeros_like(tile)).reshape(4, 64, 128)
            pst[part, half, :, :, t * 128 : t * 128 + 128] = tile

    copies = []

    def step_one(part):
        for half in range(2):
            one[part, half] = step_half(part, half)

    def step_half(part, half):
        me, to = (z, to_z) if half == 0 else (y, to_y)
        waits = [
            send(s1.at[part, half, (me + d) % 4], mid.at[part, half, me], to(d), mid.at[part, half, (me + 4 - d) % 4])
            for d in RING
        ]
        return waits, local(s1.at[part, half, me], mid.at[part, half, me])

    def step_two(part):
        for half in range(2):
            arrive(one[part, half][0])
            one[part, half][1].wait()
            me, to = (y, to_y) if half == 0 else (z, to_z)
            for d in RING:
                two.append(
                    send(
                        mid.at[part, half, :, (me + d) % 4], arr.at[part, half, me], to(d),
                        arr.at[part, half, (me + 4 - d) % 4],
                    )
                )
            copies.append(local(mid.at[part, half, :, me], arr.at[part, half, me]))

    one, two = {}, []

    def make(part):
        if part % 2 == 0:
            arrive(g0 if part == 0 else g1)
            turn(part // 2)
        arrive(child[part])
        for half in range(2):
            schur(part, half)
        if part + 2 < 4:
            child[part + 2] = send_child(part + 2)

    make(0)
    step_one(0)
    g1 = rows_two(1, g1)
    make(1)
    step_one(1)
    step_two(0)
    make(2)
    make(3)

    @pl.loop(0, 24)
    def _(i):
        source_row = tab[T_RFROM + i]
        rank, half = source_row // 8, source_row % 8 // 4
        place = source_row % 4
        tile = jnp.concatenate([pst[rank * 2, half, place], pst[rank * 2 + 1, half, place]], axis=0)
        psp[i // 6, i % 6 // 2, i % 2] = jnp.where(tab[T_ROK + i] == 1, tile, jnp.zeros_like(tile))

    y32 = pl.ds(pl.multiple_of(y * 32, 32), 32)
    f1, f2 = [], []
    for n, d in enumerate(RING):
        f1.append(send(psp.at[(z + d) % 4, :, 0], ra.at[n], to_z(d), ra.at[n]))
        f2.append(send(psp.at[:, :, 1, pl.ds((y + d) % 4 * 32, 32)], rb.at[n], to_y(d), rb.at[n]))
    step_two(1)
    arrive(f1)
    sa[...] = psp[z, :, 0] + ra[0] + ra[1] + ra[2]
    f3 = [send(sa.at[:, pl.ds((y + d) % 4 * 32, 32)], ra2.at[n], to_y(d), ra2.at[n]) for n, d in enumerate(RING)]
    arrive(f2)
    sb[...] = psp[:, :, 1, y32] + rb[0] + rb[1] + rb[2]
    f4 = [send(sb.at[(z + d) % 4], rb2.at[n], to_z(d), rb2.at[n]) for n, d in enumerate(RING)]
    step_one(2)
    arrive(f3)
    arrive(f4)
    arrive(e1)
    own_fe.wait()
    even = sa[:, y32] + ra2[0] + ra2[1] + ra2[2]
    odd = sb[z] + rb2[0] + rb2[1] + rb2[2]
    even = (fe[:, 0].astype(F32) + even.astype(F32)).astype(BF).reshape(96, 512)
    odd = (fe[:, 1].astype(F32) + odd.astype(F32)).astype(BF).reshape(96, 512)
    pp[:, 0] = jnp.dot(even, dinv[...], preferred_element_type=F32).astype(BF).reshape(3, 32, 512)
    pp[:, 1] = jnp.dot(odd, dinv[...], preferred_element_type=F32).astype(BF).reshape(3, 32, 512)
    own = local(pp, prow.at[z, :, :, y32])
    p1, p2 = [], []
    for d in RING:
        p1.append(send(pp.at[:, 0], prow.at[z, :, 0, y32], to_z(d), prow.at[(z + 4 - d) % 4, :, 0, y32]))
        p2.append(send(pp.at[:, 1], prow.at[z, :, 1, y32], to_y(d), prow.at[z, :, 1, pl.ds((y + 4 - d) % 4 * 32, 32)]))
    own.wait()
    step_one(3)
    arrive(p1)
    p3 = [
        send(prow.at[:, :, 0, y32], prow.at[:, :, 0, y32], to_y(d), prow.at[:, :, 0, pl.ds((y + 4 - d) % 4 * 32, 32)])
        for d in RING
    ]
    arrive(p2)
    p4 = [send(prow.at[z, :, 1], prow.at[z, :, 1], to_z(d), prow.at[(z + 4 - d) % 4, :, 1]) for d in RING]
    step_two(2)
    arrive(p3)
    arrive(p4)

    root = c % 8
    upper = c // 8
    n_in = sem()
    n_out = [sem() for _ in ROWS]

    def piece(q):
        return pl.ds(q * 16, 16)

    def deal(dx, dk, n):
        q = row_dev(dx, dk)
        return remote(prow.at[:, :, upper, piece(q)], pcol.at[:, :, piece(q)], n, n_in, (q, c))

    @pl.when(r == root)
    def _():
        for (dx, dk), n in zip(ROWS, n_out):
            deal(dx, dk, n).start()
        copy = pltpu.make_async_copy(prow.at[:, :, upper, piece(r)], pcol.at[:, :, piece(r)], lsem.at[N_SEMS - 2])
        copy.start()
        copy.wait()
        for (dx, dk), n in zip(ROWS, n_out):
            deal(dx, dk, n).wait_send()

    @pl.when(r != root)
    def _():
        remote(pcol.at[:, :, piece(r)], pcol.at[:, :, piece(r)], n_in, n_in, (r, c)).wait_recv()

    q1 = [
        send(
            pcol.at[:, :, piece(r)], pcol.at[:, :, piece(r)], (row_dev(d, 0), c), pcol.at[:, :, piece(row_from(d, 0))]
        )
        for d in RING
    ]
    step_two(3)
    arrive(q1)
    q2 = [
        send(
            pcol.at[:, :, piece(2 * q + k)], pcol.at[:, :, piece(2 * q + k)], sibling,
            pcol.at[:, :, piece(2 * q + 1 - k)],
        )
        for q in range(4)
    ]

    arrive(q2)
    arrive(two)
    for copy in copies:
        copy.wait()
    for copy in pending:
        copy.wait_send()


def update(tab, front, *refs):
    arrs, (prow, pcol, out, panel, right) = refs[:8], refs[8:]
    r, c = lax.axis_index("row"), lax.axis_index("col")
    step = pl.program_id(0)

    @pl.when(step == 0)
    def _():
        for j in range(12):
            tile = pcol[j // 3, j % 3]
            if j == 0:
                tile = jnp.where(c >= 4, tile, jnp.zeros_like(tile))
            right[:, j * 128 : j * 128 + 128] = tile.T

    rows = prow[...].reshape(512, 512)
    pick = (lax.broadcasted_iota(jnp.int32, (32, 512), 1) - 32 * c) == lax.broadcasted_iota(jnp.int32, (32, 512), 0)
    chosen = lax.dot_general(
        jnp.where(pick, 1.0, 0.0).astype(BF), rows, (((1,), (1,)), ((), ())), preferred_element_type=F32
    ).astype(BF)
    for b in range(4):
        panel[b] = chosen[:, b * 128 : b * 128 + 128]
    trailing = jnp.logical_or(step > 0, r >= 4)
    rows = jnp.concatenate([jnp.where(trailing, rows[0:128], jnp.zeros_like(rows[0:128])), rows[128:512]], axis=0)
    for n in range(6):
        prod = jnp.dot(rows, right[:, n * 256 : n * 256 + 256], preferred_element_type=F32)
        for e in range(2):
            for b in range(4):
                j = 2 * n + e
                _, _, _, major, minor, ok = arrived_place(tab, 4 * step + b, j)
                for p in range(2):
                    tile = arrs[2 * b + p][0, 0, major, minor]
                    lines = slice(p * 64, p * 64 + 64)
                    ext = (
                        front[b, j, lines].astype(F32) + jnp.where(ok, tile, jnp.zeros_like(tile)).astype(F32)
                    ).astype(BF)
                    term = prod[b * 128 + p * 64 : b * 128 + p * 64 + 64, e * 128 : e * 128 + 128]
                    out[b, j, lines] = (ext.astype(F32) - term).astype(BF)


def arrivals(b, p):
    def index(step, tab):
        source_row = tab[T_RFROM + 4 * step + b]
        return (source_row // 8 * 2 + p, source_row % 8 // 4, 0, 0, source_row % 4, 0)

    return pl.BlockSpec((1, 1, 4, 4, 64, 128), index)


def body(child_update, child_panel, front, diag_inverse, parent_tile):
    tab = tables(parent_tile, lax.axis_index("row"), lax.axis_index("col"))
    u = child_update.reshape(2, 2, 4, 4, 256, 128)
    gt = child_panel.reshape(16, 128, 32).transpose(0, 2, 1)
    tiles = front.reshape(24, 128, 12, 128).transpose(0, 2, 1, 3)
    vmem, anywhere = pl.BlockSpec(memory_space=pltpu.VMEM), pl.BlockSpec(memory_space=pl.ANY)
    smem = pl.BlockSpec(memory_space=pltpu.SMEM)
    arr, prow, pcol = pl.pallas_call(
        exchange,
        out_shape=(
            jax.ShapeDtypeStruct((4, 2, 4, 4, 256, 128), BF),
            jax.ShapeDtypeStruct((4, 3, 2, 128, 512), BF),
            jax.ShapeDtypeStruct((4, 3, 128, 512), BF),
        ),
        in_specs=[smem, anywhere, vmem, anywhere, vmem],
        out_specs=(anywhere, anywhere, anywhere),
        scratch_shapes=[
            pltpu.VMEM((8, 2, 1024, 128), BF),
            pltpu.VMEM((8, 2, 1024, 128), BF),
            pltpu.VMEM((8, 4, 32, 128), BF),
            pltpu.VMEM((8, 4, 32, 128), BF),
            pltpu.VMEM((2, 8, 512, 128), BF),
            pltpu.VMEM((4, 8, 64, 512), BF),
            pltpu.VMEM((4, 4, 32, 128), BF),
            pltpu.VMEM((4, 4, 32, 128), BF),
            pltpu.VMEM((8, 4, 4, 32, 128), BF),
            pltpu.VMEM((512, 1024), BF),
            pltpu.VMEM((512, 1024), BF),
            pltpu.VMEM((2048, 128), F32),
            pltpu.VMEM((8, 256, 128), BF),
            pltpu.VMEM((4, 2, 4, 4, 256, 128), BF),
            pltpu.VMEM((4, 2, 4, 4, 256, 128), BF),
            pltpu.VMEM((4, 2, 4, 64, 512), BF),
            pltpu.VMEM((4, 3, 2, 128, 512), BF),
            pltpu.VMEM((3, 3, 128, 512), BF),
            pltpu.VMEM((3, 128, 512), BF),
            pltpu.VMEM((3, 3, 32, 512), BF),
            pltpu.VMEM((3, 4, 3, 32, 512), BF),
            pltpu.VMEM((4, 3, 32, 512), BF),
            pltpu.VMEM((3, 3, 32, 512), BF),
            pltpu.VMEM((3, 2, 128, 128), BF),
            pltpu.VMEM((3, 2, 32, 512), BF),
            pltpu.VMEM((3, 2, 32, 512), BF),
            pltpu.SemaphoreType.DMA((N_SEMS,)),
            pltpu.SemaphoreType.DMA((N_SEMS,)),
            pltpu.SemaphoreType.DMA((N_SEMS,)),
        ],
        compiler_params=pltpu.CompilerParams(collective_id=0, has_side_effects=True, vmem_limit_bytes=KERNEL_VMEM),
        name="exchange",
    )(tab, u, gt, tiles.reshape(4, 3, 2, 12, 128, 128), diag_inverse)
    updated, panel = pl.pallas_call(
        update,
        grid_spec=pltpu.PrefetchScalarGridSpec(
            num_scalar_prefetch=1,
            grid=(6,),
            in_specs=[
                pl.BlockSpec((4, 12, 128, 128), lambda s, t: (s, 0, 0, 0)),
                *[arrivals(b, p) for b in range(4) for p in range(2)],
                pl.BlockSpec((4, 128, 512), lambda s, t: (s, 0, 0)),
                pl.BlockSpec((4, 3, 128, 512), lambda s, t: (0, 0, 0, 0)),
            ],
            out_specs=[
                pl.BlockSpec((4, 12, 128, 128), lambda s, t: (s, 0, 0, 0)),
                pl.BlockSpec((4, 32, 128), lambda s, t: (s, 0, 0)),
            ],
            scratch_shapes=[pltpu.VMEM((512, 1536), BF)],
        ),
        out_shape=(jax.ShapeDtypeStruct((24, 12, 128, 128), BF), jax.ShapeDtypeStruct((24, 32, 128), BF)),
        compiler_params=pltpu.CompilerParams(vmem_limit_bytes=46 << 20),
        name="update",
    )(tab, tiles, *[arr] * 8, prow.reshape(24, 128, 512), pcol)
    return (
        panel.transpose(0, 2, 1).reshape(24, 1, 128, 1, 32),
        updated.transpose(0, 2, 1, 3).reshape(24, 1, 128, 12, 1, 128),
    )


def solution(mesh):
    return jax.shard_map(
        body,
        mesh=mesh,
        in_specs=(
            P(None, "row", None, None, "col", None),
            P(None, "row", None, "col"),
            P(None, "row", None, None, "col", None),
            P(),
            P(),
        ),
        out_specs=(P(None, "row", None, "col", None), P(None, "row", None, None, "col", None)),
        check_vma=False,
    )
```
